256 devices in a mesh: dp: 32 (over x, y, core), seq: 8 (over z).
Axes of the slice: x: 4, y: 4, z: 8, core: 2. Of those that a mesh axis runs over, the one named last changes fastest.
Arguments:
- queries: bfloat16 [64, 1024, 2048], P('dp', 'seq'), may hold values from -10 to 10
- key_states: bfloat16 [64, 1024, 512], P('dp', 'seq'), may hold values from -10 to 10
- value_states: bfloat16 [64, 1024, 512], P('dp', 'seq'), may hold values from -6 to 6
- grad_out: bfloat16 [64, 1024, 2048], P('dp', None, 'seq'), may hold values from -6 to 6
- doc_ids: int32 [64, 1024], replicated, may hold values from 0 to 2, never falling along the last dimension, each value on 1 to 768 neighbouring positions
- partner: int32 [32], replicated, may hold values from 0 to 31, as said below
- swap_rows: int32 [32, 1], replicated, may hold values from 0 to 1, as said below
Outputs:
- attended: bfloat16 [64, 1024, 2048], P('dp', None, 'seq')
- grad_queries: bfloat16 [64, 1024, 2048], P('dp', 'seq')
- grad_keys: bfloat16 [64, 1024, 512], P('dp', 'seq')
- grad_values: bfloat16 [64, 1024, 512], P('dp', 'seq')
The draws below stay inside these ranges and needn't reach their ends.
Inputs may be any that keep to these rules, and one draw needn't show every extreme that they name: partner[partner[g]] == g and partner[g] != g. `swap_rows`: the 1 entries of one group are distinct.
All inputs are finite; a program needn't handle non-finite values.
Results may differ from the reference program's by a relative error of at most 0.0075.
Values may be sent and summed in bfloat16 or wider, within the bound.
No kernel may reach another device: no remote copies, remote signals or barrier semaphores. Data moves between devices by JAX's collectives and lax.ppermute only.
A program may use at most 64 MiB of HBM per device.

```python
import math
import jax
import jax.numpy as jnp
import numpy as np
from jax import lax

QH = 16
KVH = 4
HD = 128
LENGTH = 1024
ROWS = 2
DOCS = 3
ALL_ROWS = 64
N_DP = 32
N_SEQ = 8


def draw_queries(key, part):
    key = jax.random.fold_in(key, 3)
    sample = jnp.clip(jax.random.normal(key, (ROWS * N_DP, LENGTH, QH, HD), jnp.float32), -6.0, 6.0)
    return sample.reshape(ROWS * N_DP, LENGTH, QH * HD).astype(jnp.bfloat16)


def draw_key_states(key, part):
    key = jax.random.fold_in(key, 5)
    sample = jnp.clip(jax.random.normal(key, (ROWS * N_DP, LENGTH, KVH, HD), jnp.float32), -6.0, 6.0)
    return sample.reshape(ROWS * N_DP, LENGTH, KVH * HD).astype(jnp.bfloat16)


def draw_partner(key, part):
    key = jax.random.fold_in(key, 7)
    order = jax.random.permutation(key, N_DP).astype(jnp.int32)
    evens = order[0::2]
    odds = order[1::2]
    result = jnp.zeros((N_DP,), jnp.int32).at[evens].set(odds).at[odds].set(evens)
    return result


def draw_swap_rows(key, part):
    key = jax.random.fold_in(key, 11)
    group_keys = jax.random.split(key, N_DP)
    picked = jax.vmap(lambda single: jax.random.permutation(single, ROWS)[:ROWS // 2])(group_keys)
    return picked.astype(jnp.int32)


def level_of(stream_key, shape, pieces, least, top_value):
    def one(dim, parts):
        draws = jax.random.uniform(jax.random.fold_in(jax.random.fold_in(stream_key, 6), dim), (parts,), jnp.float32, least / len(pieces), top_value / len(pieces))
        return jnp.repeat(jnp.exp(draws), shape[dim] // parts).reshape((-1,) + (1,) * (len(shape) - dim - 1))

    gain = one(*pieces[0])
    for cut in pieces[1:]:
        gain = gain * one(*cut)
    return gain


def length_profile(amount, total, limit, lean):
    portions = [(1 << 20) // math.isqrt(rank ** lean) + 1 for rank in range(2, amount + 1)]
    surplus, counts = total - limit - (amount - 1), [1] * (amount - 1)
    while surplus > 0:
        movable = [i for i in range(amount - 1) if counts[i] < limit]
        whole, left = sum([portions[i] for i in movable]), surplus
        for i in movable:
            extra = min(limit - counts[i], max(1, left * portions[i] // whole), surplus)
            counts[i] = counts[i] + extra
            surplus = surplus - extra
    return np.array([limit] + counts)


def uneven(stream_key, amount, total, bound, lean):
    if amount == 2:
        one = jax.random.randint(stream_key, (), max(1, total - bound), min(bound, total - 1) + 1)
        return jnp.stack([one, total - one])
    lengths = jnp.asarray(length_profile(amount, total, bound, lean), jnp.int32)
    couples = (amount - 1) // 2
    donor, receiver = lengths[1:1 + 2 * couples:2], lengths[2:2 + 2 * couples:2]
    slack = jnp.minimum(donor - 1, bound - receiver)
    shifted = jax.random.randint(jax.random.fold_in(stream_key, 1), (couples,), 0, 1 << 20) % (slack + 1)
    lengths = lengths.at[1:1 + 2 * couples:2].set(donor - shifted).at[2:2 + 2 * couples:2].set(receiver + shifted)
    return lengths[jax.random.permutation(jax.random.fold_in(stream_key, 2), amount)]


def normal_values(rng, dims, width, limit, shards=(), held_as=jnp.bfloat16):
    drawn = width * jax.random.normal(rng, dims, jnp.float32)
    if shards:
        drawn = drawn * level_of(rng, dims, shards, -0.22, 0.18)
    return jnp.clip(drawn, -limit, limit).astype(held_as)


def setup_inputs(seed: int = 0) -> dict:
    splits = jax.random.split(jax.random.key(seed), 8)
    return {
        "queries": draw_queries(jax.random.fold_in(splits[7], 71), 0),
        "key_states": draw_key_states(jax.random.fold_in(splits[7], 71), 0),
        "value_states": normal_values(splits[2], (ALL_ROWS, LENGTH, KVH * HD), 1.0, 6.0, ((0, 32), (1, 8))),
        "grad_out": normal_values(splits[3], (ALL_ROWS, LENGTH, QH * HD), 1.0, 6.0, ((0, 32), (2, 8))),
        "doc_ids": jax.vmap(lambda own: jnp.searchsorted(jnp.cumsum(uneven(own, DOCS, LENGTH, 3 * LENGTH // 4, 2)), jnp.arange(LENGTH), side="right"))(jax.random.split(splits[4], ALL_ROWS)).reshape((ALL_ROWS, LENGTH)).astype(jnp.int32),
        "partner": draw_partner(jax.random.fold_in(splits[7], 71), 0),
        "swap_rows": draw_swap_rows(jax.random.fold_in(splits[7], 71), 0),
    }


def head_terms(query_head, key_head, value_head, grad_head, allowed, scaling):
    scores = jnp.dot(query_head, key_head.T, preferred_element_type=jnp.float32) * scaling
    scores = jnp.where(allowed, scores, -1e30)
    row_max = jnp.max(scores, axis=1, keepdims=True)
    exponent = jnp.where(allowed, jnp.exp(scores - row_max), 0.0)
    weights = exponent / jnp.sum(exponent, axis=1, keepdims=True)
    rounded = weights.astype(jnp.bfloat16)
    attended = jnp.dot(rounded, value_head, preferred_element_type=jnp.float32).astype(jnp.bfloat16)
    grad_probs = jnp.dot(grad_head, value_head.T, preferred_element_type=jnp.float32)
    inner_sum = jnp.sum(weights * grad_probs, axis=1, keepdims=True)
    dscore = (weights * (grad_probs - inner_sum) * scaling).astype(jnp.bfloat16)
    grad_q = jnp.dot(dscore, key_head, preferred_element_type=jnp.float32).astype(jnp.bfloat16)
    grad_k = jnp.dot(dscore.T, query_head, preferred_element_type=jnp.float32)
    grad_v = jnp.dot(rounded.T, grad_head, preferred_element_type=jnp.float32)
    return attended, grad_q, grad_k, grad_v


def reference(queries, key_states, value_states, grad_out, doc_ids, partner, swap_rows):
    slots = (jnp.arange(N_DP, dtype=jnp.int32)[:, None] * ROWS + swap_rows).reshape(-1).astype(jnp.int32)
    anchor = (partner[:, None] * ROWS + jnp.take(swap_rows, partner, axis=0)).reshape(-1).astype(jnp.int32)
    source = jnp.arange(ROWS * N_DP, dtype=jnp.int32).at[slots].set(anchor)
    scaling = float(HD) ** -0.5
    group_size = QH // KVH
    set_size = QH // N_SEQ
    position = jnp.arange(LENGTH, dtype=jnp.int32)

    def row_terms(inputs):
        query_row, key_row, value_row, grad_row, doc_row = inputs
        allowed = (doc_row[:, None] == doc_row[None, :]) & (position[None, :] <= position[:, None])
        attended_list, grad_q_list, key_sums, value_sums = [], [], [], []
        for kv_head in range(KVH):
            key_head = key_row[:, kv_head * HD:(kv_head + 1) * HD]
            value_head = value_row[:, kv_head * HD:(kv_head + 1) * HD]
            key_total = jnp.zeros((LENGTH, HD), jnp.float32)
            value_total = jnp.zeros((LENGTH, HD), jnp.float32)
            for first in range(0, group_size, set_size):
                key_set = jnp.zeros((LENGTH, HD), jnp.float32)
                value_set = jnp.zeros((LENGTH, HD), jnp.float32)
                for head in range(kv_head * group_size + first, kv_head * group_size + first + set_size):
                    part_att, part_q, part_k, part_v = head_terms(
                        query_row[:, head * HD:(head + 1) * HD], key_head, value_head,
                        grad_row[:, head * HD:(head + 1) * HD], allowed, scaling)
                    attended_list.append(part_att)
                    grad_q_list.append(part_q)
                    key_set = key_set + part_k
                    value_set = value_set + part_v
                key_total = key_total + lax.optimization_barrier(key_set.astype(jnp.bfloat16)).astype(jnp.float32)
                value_total = value_total + lax.optimization_barrier(value_set.astype(jnp.bfloat16)).astype(jnp.float32)
            key_sums.append(key_total.astype(jnp.bfloat16))
            value_sums.append(value_total.astype(jnp.bfloat16))
        return (jnp.concatenate(attended_list, axis=1), jnp.concatenate(grad_q_list, axis=1),
                jnp.concatenate(key_sums, axis=1), jnp.concatenate(value_sums, axis=1))

    balanced = (jnp.take(queries, source, axis=0), jnp.take(key_states, source, axis=0),
                jnp.take(value_states, source, axis=0), grad_out, jnp.take(doc_ids, source, axis=0))
    attended, grad_q_rows, grad_k_rows, grad_v_rows = lax.map(row_terms, balanced)
    grad_queries = jnp.zeros_like(queries).at[source].set(grad_q_rows)
    grad_keys = jnp.zeros_like(key_states).at[source].set(grad_k_rows)
    grad_values = jnp.zeros_like(value_states).at[source].set(grad_v_rows)
    return (attended, grad_queries, grad_keys, grad_values)
```

```python
import functools

import jax
import jax.numpy as jnp
from jax import lax
from jax.experimental import pallas as pl
from jax.experimental.pallas import tpu as pltpu
from jax.sharding import PartitionSpec as P

QH = 16
KVH = 4
HD = 128
BLOCK = 256
FAR = -1e30
VMEM = pl.BlockSpec(memory_space=pltpu.VMEM)
SMEM = pl.BlockSpec(memory_space=pltpu.SMEM)
PARAMS = pltpu.CompilerParams(vmem_limit_bytes=48 * 1024 * 1024)


def dot(a, b, dims=((1,), (0,))):
    return lax.dot_general(a, b, (dims, ((), ())), preferred_element_type=jnp.float32)


def pack_kernel(seq, where, q_ref, k_ref, v_ref, *outs):
    me = where[0]
    for unit in range(2):
        row = where[1 + unit]
        for s in range(seq):
            to = lax.rem(me + s, seq)
            out = outs[unit * seq + s]
            out[:, 0:256] = q_ref[row, :, pl.ds(pl.multiple_of(to * 256, 256), 256)]
            kv = pl.ds(pl.multiple_of((to // 2) * HD, HD), HD)
            out[:, 256:384] = k_ref[row, :, kv]
            out[:, 384:512] = v_ref[row, :, kv]


def pack(where, q, k, v, seq):
    tok = q.shape[1]
    return pl.pallas_call(
        functools.partial(pack_kernel, seq),
        out_shape=[jax.ShapeDtypeStruct((tok, 512), q.dtype)] * (2 * seq),
        in_specs=[SMEM, VMEM, VMEM, VMEM],
        out_specs=[VMEM] * (2 * seq),
        compiler_params=PARAMS,
        name="pack",
    )(where, q, k, v)


def row_kernel(seq, tok, where, *refs):
    xs, refs = refs[:seq], refs[seq:]
    do_ref, qm_ref, km_ref, att_ref = refs[:4]
    gs, refs = refs[4 : 4 + seq], refs[4 + seq :]
    qa, ka, v_s, kt, vt, dk, dv, grads = refs
    me = where[0]
    length = seq * tok
    scaling = float(HD) ** (-0.5)
    to_log2 = scaling * 1.4426950408889634
    for s in range(seq):
        at = pl.ds(pl.multiple_of(lax.rem(me + seq - s, seq) * tok, tok), tok)
        qa[0, at, 0:HD] = xs[s][:, 0:128]
        qa[1, at, 0:HD] = xs[s][:, 128:256]
        ka[at, 0:HD] = xs[s][:, 256:384]
        v_s[at, :] = xs[s][:, 384:512]
    qa[0, :, HD:] = qm_ref[...]
    qa[1, :, HD:] = qm_ref[...]
    ka[:, HD:] = km_ref[...]
    kt[...] = ka[:, 0:HD].T
    vt[...] = v_s[...].T
    dk[...] = jnp.zeros_like(dk)
    dv[...] = jnp.zeros_like(dv)
    steps = length // BLOCK
    key_at = lax.broadcasted_iota(jnp.int32, (BLOCK, BLOCK), 0)
    query_at = lax.broadcasted_iota(jnp.int32, (BLOCK, BLOCK), 1)
    causal = key_at <= query_at
    for i in range(steps):
        rows = slice(i * BLOCK, (i + 1) * BLOCK)
        for h in range(2):
            cols = slice(h * HD, (h + 1) * HD)
            query = qa[h, rows, :]
            scores = []
            for b in range(i + 1):
                block = dot(ka[b * BLOCK : (b + 1) * BLOCK, :], query, ((1,), (1,)))
                if b == i:
                    block = jnp.where(causal, block, FAR)
                scores.append(block)
            top = functools.reduce(
                jnp.maximum, [jnp.max(block, axis=0, keepdims=True) for block in scores]
            )
            expo = [jnp.exp2((block - top) * to_log2) for block in scores]
            total = sum(jnp.sum(block, axis=0, keepdims=True) for block in expo)
            inverse = 1.0 / total
            weights = [block * inverse for block in expo]
            probs = [block.astype(jnp.bfloat16) for block in weights]
            out_t = sum(
                dot(vt[:, b * BLOCK : (b + 1) * BLOCK], probs[b]) for b in range(i + 1)
            )
            att_ref[rows, cols] = out_t.T.astype(jnp.bfloat16)
            grad = do_ref[rows, cols]
            grad_t = grad.T
            inner = jnp.sum(grad_t.astype(jnp.float32) * out_t, axis=0, keepdims=True)
            dq_t = jnp.zeros((HD, BLOCK), jnp.float32)
            for b in range(i + 1):
                keys = slice(b * BLOCK, (b + 1) * BLOCK)
                grad_probs = dot(v_s[keys, :], grad_t)
                dscore = (weights[b] * (grad_probs - inner)).astype(jnp.bfloat16)
                dq_t = dq_t + dot(kt[:, keys], dscore)
                dk[keys, :] += dot(dscore, query[:, 0:HD])
                dv[keys, :] += dot(probs[b], grad)
            grads[rows, cols] = (dq_t * scaling).T.astype(jnp.bfloat16)
    grads[:, 256:384] = (dk[...] * scaling).astype(jnp.bfloat16)
    grads[:, 384:512] = dv[...].astype(jnp.bfloat16)
    for s in range(seq):
        at = pl.ds(pl.multiple_of(lax.rem(me + s, seq) * tok, tok), tok)
        gs[s][...] = grads[at, :]


def row_call(where, xs, grad, query_mark, key_mark, name):
    seq, tok = len(xs), xs[0].shape[0]
    length = seq * tok
    bf16, f32 = jnp.bfloat16, jnp.float32
    flops = 6 * 2 * 2 * length * length * HD
    out = pl.pallas_call(
        functools.partial(row_kernel, seq, tok),
        out_shape=[jax.ShapeDtypeStruct((length, 256), bf16)]
        + [jax.ShapeDtypeStruct((tok, 512), bf16)] * seq,
        in_specs=[SMEM] + [VMEM] * (seq + 3),
        out_specs=[VMEM] * (seq + 1),
        scratch_shapes=[
            pltpu.VMEM((2, length, 256), bf16),
            pltpu.VMEM((length, 256), bf16),
            pltpu.VMEM((length, HD), bf16),
            pltpu.VMEM((HD, length), bf16),
            pltpu.VMEM((HD, length), bf16),
            pltpu.VMEM((length, HD), f32),
            pltpu.VMEM((length, HD), f32),
            pltpu.VMEM((length, 512), bf16),
        ],
        compiler_params=PARAMS,
        cost_estimate=pl.CostEstimate(
            flops=flops, bytes_accessed=3 * 2**20, transcendentals=2 * length * length
        ),
        name=name,
    )(where, *xs, grad, query_mark, key_mark)
    return out[0], out[1:]


def unpack_kernel(seq, where, *refs):
    parts, (gq, gk, gv) = refs[: 2 * seq], refs[2 * seq :]
    me = where[0]
    for unit in range(2):
        row = where[1 + unit]
        mine = parts[unit * seq : (unit + 1) * seq]
        for s in range(seq):
            origin = lax.rem(me + seq - s, seq)
            gq[row, :, pl.ds(pl.multiple_of(origin * 256, 256), 256)] = mine[s][:, 0:256]
        even = lax.rem(me, 2) == 0
        for s in range(0, seq, 2):
            origin = lax.rem(me + seq - s, seq)
            near = mine[s]
            left, right = mine[(s + seq - 1) % seq], mine[(s + 1) % seq]
            at = pl.ds(pl.multiple_of((origin // 2) * HD, HD), HD)
            for ref, cols in ((gk, slice(256, 384)), (gv, slice(384, 512))):
                other = jnp.where(even, left[:, cols], right[:, cols])
                both = near[:, cols].astype(jnp.float32) + other.astype(jnp.float32)
                ref[row, :, at] = both.astype(jnp.bfloat16)


def unpack(where, parts, seq):
    tok = parts[0].shape[0]
    bf16 = jnp.bfloat16
    return pl.pallas_call(
        functools.partial(unpack_kernel, seq),
        out_shape=[
            jax.ShapeDtypeStruct((2, tok, QH * HD), bf16),
            jax.ShapeDtypeStruct((2, tok, KVH * HD), bf16),
            jax.ShapeDtypeStruct((2, tok, KVH * HD), bf16),
        ],
        in_specs=[SMEM] + [VMEM] * (2 * seq),
        out_specs=[VMEM] * 3,
        compiler_params=PARAMS,
        name="unpack",
    )(where, *parts)


def shifted(arrays, seq):
    out = [arrays[0]]
    for s in range(1, seq):
        out.append(lax.ppermute(arrays[s], "seq", [(d, (d + s) % seq) for d in range(seq)]))
    return out


def swapped(row, partner):
    groups = lax.axis_size("dp")
    shape = row.shape
    pieces = row.reshape(groups, shape[0] // groups, shape[1])
    spread = lax.all_to_all(pieces, "dp", 0, 0, tiled=True)
    routed = jnp.take(spread, partner, axis=0)
    return lax.all_to_all(routed, "dp", 0, 0, tiled=True).reshape(shape)


def per_device(queries, key_states, value_states, grad_out, doc_ids, partner, swap_rows):
    seq = lax.axis_size("seq")
    group = lax.axis_index("dp")
    me = lax.axis_index("seq").astype(jnp.int32)
    moving = swap_rows[group, 0]
    staying = 1 - moving
    where = jnp.stack([me, staying, moving])
    docs = lax.dynamic_slice_in_dim(doc_ids, group * 2, 2, 0)
    docs = jnp.stack([docs[staying], docs[moving]])
    lanes = jnp.arange(HD, dtype=jnp.int32)
    same = docs[:, :, None] == lanes
    key_mark = same.astype(jnp.bfloat16)
    query_mark = jnp.where(same, 0.0, FAR).astype(jnp.bfloat16)

    grad_stay = lax.dynamic_index_in_dim(grad_out, staying, 0, False)
    grad_move = swapped(lax.dynamic_index_in_dim(grad_out, moving, 0, False), partner)
    sent = pack(where, queries, key_states, value_states, seq)
    first = shifted(sent[:seq], seq)
    second = shifted(sent[seq:], seq)
    att_move, back_move = row_call(where, second, grad_move, query_mark[1], key_mark[1], "moving")
    att_stay, back_stay = row_call(where, first, grad_stay, query_mark[0], key_mark[0], "staying")
    att_move = swapped(att_move, partner)
    got_stay = shifted(back_stay, seq)
    got_move = shifted(back_move, seq)
    gq, gk, gv = unpack(where, list(got_stay) + list(got_move), seq)
    order = (moving == 0)
    attended = jnp.where(
        order, jnp.stack([att_move, att_stay]), jnp.stack([att_stay, att_move])
    )
    return attended, gq, gk, gv


def solution(mesh):
    return jax.shard_map(
        per_device,
        mesh=mesh,
        in_specs=(
            P("dp", "seq", None),
            P("dp", "seq", None),
            P("dp", "seq", None),
            P("dp", None, "seq"),
            P(),
            P(),
            P(),
        ),
        out_specs=(
            P("dp", None, "seq"),
            P("dp", "seq", None),
            P("dp", "seq", None),
            P("dp", "seq", None),
        ),
        check_vma=False,
    )
```

```python
import functools

import jax
import jax.numpy as jnp
from jax import lax
from jax.experimental import pallas as pl
from jax.experimental.pallas import tpu as pltpu
from jax.sharding import PartitionSpec as P

QH = 16
KVH = 4
HD = 128
BLOCK = 256
FAR = -1e30
ORDER_IN = (1, 7, 4, 3, 5, 2, 6)
ORDER_OUT = (3, 5, 2, 6, 4, 1, 7)
ANY = pl.BlockSpec(memory_space=pl.ANY)
HBM = pl.BlockSpec(memory_space=pltpu.HBM)
SMEM = pl.BlockSpec(memory_space=pltpu.SMEM)
MIB = 1024 * 1024
BF16 = jnp.bfloat16


def dot(a, b, dims=((1,), (0,))):
    return lax.dot_general(a, b, (dims, ((), ())), preferred_element_type=jnp.float32)


def part(index, size):
    return pl.ds(pl.multiple_of(index * size, size), size)


def places(swap_rows):
    moving = swap_rows[0, lax.axis_index("dp")]
    return lax.axis_index("seq"), 1 - moving, moving


class Copies:
    def __init__(self, sems):
        self.sems, self.all = sems, []

    def start(self, source, target):
        copy = pltpu.make_async_copy(source, target, self.sems.at[len(self.all)])
        copy.start()
        self.all.append(copy)
        return copy

    def wait(self, begin=0, end=None):
        for copy in self.all[begin:end]:
            copy.wait()


def call(kernel, operands, outs, scratch, name, aliases=None, limit=60, flops=0, nbytes=2 * MIB):
    return pl.pallas_call(
        kernel,
        out_shape=outs,
        in_specs=[SMEM] + [HBM] * (len(operands) - 1),
        out_specs=[HBM] * len(outs),
        scratch_shapes=scratch,
        input_output_aliases=aliases or {},
        compiler_params=pltpu.CompilerParams(vmem_limit_bytes=limit * MIB),
        cost_estimate=pl.CostEstimate(flops=flops, bytes_accessed=nbytes, transcendentals=0),
        name=name,
    )(*operands)


def pack_kernel(seq, where, q_ref, k_ref, v_ref, grad_ref, *refs):
    outs, grad_out, (chunks, grad, sems_in, sems_out) = refs[:seq], refs[seq], refs[-4:]
    me, *rows = places(where)
    loads, stores = Copies(sems_in), Copies(sems_out)
    order = (*ORDER_IN, 0)
    for s in order:
        to = lax.rem(me + s, seq)
        head, chunk = part(to // 2, HD), chunks.at[s]
        loads.start(q_ref.at[:, :, part(to, 256)], chunk.at[:, :, pl.ds(0, 256)])
        loads.start(k_ref.at[:, :, head], chunk.at[:, :, pl.ds(256, HD)])
        loads.start(v_ref.at[:, :, head], chunk.at[:, :, pl.ds(384, HD)])
        if s == order[0]:
            loads.start(grad_ref.at[rows[1]], grad)
    at = 0
    for s in order:
        loads.wait(at, at + 3)
        stores.start(chunks.at[s], outs[s])
        at += 3
        if s == order[0]:
            loads.wait(at, at + 1)
            stores.start(grad, grad_out)
            at += 1
    stores.wait()


def pack(where, q, k, v, grad, seq):
    tok, length = q.shape[1], grad.shape[1]
    out = call(
        functools.partial(pack_kernel, seq),
        (where, q, k, v, grad),
        [jax.ShapeDtypeStruct((2, tok, 512), BF16)] * seq
        + [jax.ShapeDtypeStruct((length, 256), BF16)],
        [
            pltpu.VMEM((seq, 2, tok, 512), BF16),
            pltpu.VMEM((length, 256), BF16),
            pltpu.SemaphoreType.DMA((3 * seq + 1,)),
            pltpu.SemaphoreType.DMA((seq + 1,)),
        ],
        "pack",
    )
    return out[:seq], out[seq]


def rows_kernel(seq, tok, where, *refs):
    xs, refs = dict(zip((0, *ORDER_IN), refs)), refs[seq:]
    grad_whole, grad_row, marks, att_whole, att_row = refs[0], refs[1], refs[2:6], refs[6], refs[7]
    gs, refs = refs[8 : 8 + seq], refs[8 + seq :]
    x_s, ka, qm, do, kt, vt, dk, dv, att, grads, sems_in, sems_out = refs
    me, *rows_at = places(where)
    length = seq * tok
    steps = length // BLOCK
    per = BLOCK // tok
    scaling = float(HD) ** (-0.5)
    to_log2 = scaling * 1.4426950408889634
    grad_refs = grad_whole.at[rows_at[0]], grad_row
    att_refs = att_whole.at[rows_at[0]], att_row

    def chunk_copy(unit, s, origin):
        return pltpu.make_async_copy(
            xs[s].at[rows_at[unit]], x_s.at[unit, part(origin, tok)], sems_in.at[unit, origin]
        )

    def whole_copies(unit):
        every = [
            (marks[2 * unit], qm.at[unit]),
            (marks[2 * unit + 1], ka.at[unit, :, pl.ds(HD, HD)]),
            (grad_refs[unit], do.at[unit]),
        ]
        return [
            pltpu.make_async_copy(source, target, sems_in.at[unit, seq + n])
            for n, (source, target) in enumerate(every)
        ]

    for unit in range(2):
        for copy in whole_copies(unit):
            copy.start()
        for s in range(seq):
            chunk_copy(unit, s, lax.rem(me + seq - s, seq)).start()
    key_at = lax.broadcasted_iota(jnp.int32, (BLOCK, BLOCK), 0)
    query_at = lax.broadcasted_iota(jnp.int32, (BLOCK, BLOCK), 1)
    causal = key_at <= query_at
    stores = Copies(sems_out)
    for unit, i in [(unit, i) for unit in range(2) for i in range(steps)]:
        rows = slice(i * BLOCK, (i + 1) * BLOCK)
        keys = [slice(b * BLOCK, (b + 1) * BLOCK) for b in range(i + 1)]
        if i == 0:
            for copy in whole_copies(unit):
                copy.wait()
        for origin in range(i * per, (i + 1) * per):
            chunk_copy(unit, 0, origin).wait()
        ka[unit, rows, 0:HD] = x_s[unit, rows, 256:384]
        kt[unit, :, rows] = x_s[unit, rows, 256:384].T
        vt[unit, :, rows] = x_s[unit, rows, 384:512].T
        mark = qm[unit, rows, :]
        plain = [x_s[unit, rows, h * HD : (h + 1) * HD] for h in range(2)]
        queries = [jnp.concatenate([query, mark], axis=1) for query in plain]
        gradients = [do[unit, rows, h * HD : (h + 1) * HD] for h in range(2)]
        scores, grad_probs = [], []
        for h in range(2):
            blocks = [dot(ka[unit, key, :], queries[h], ((1,), (1,))) for key in keys]
            blocks[i] = jnp.where(causal, blocks[i], FAR)
            scores.append(blocks)
        for h in range(2):
            grad_t = gradients[h].T
            grad_probs.append([dot(x_s[unit, key, 384:512], grad_t) for key in keys])
        all_probs, all_dscore = [], []
        for h in range(2):
            cols = slice(h * HD, (h + 1) * HD)
            top = functools.reduce(
                jnp.maximum, [jnp.max(block, axis=0, keepdims=True) for block in scores[h]]
            )
            expo = [jnp.exp2((block - top) * to_log2) for block in scores[h]]
            total = sum(jnp.sum(block, axis=0, keepdims=True) for block in expo)
            inverse = 1.0 / total
            weights = [block * inverse for block in expo]
            probs = [block.astype(BF16) for block in weights]
            out_t = sum(dot(vt[unit, :, key], probs[b]) for b, key in enumerate(keys))
            att[unit, rows, cols] = out_t.T.astype(BF16)
            grad_t = gradients[h].T.astype(jnp.float32)
            inner = jnp.sum(grad_t * out_t, axis=0, keepdims=True)
            dscore = [
                (weights[b] * (grad_probs[h][b] - inner)).astype(BF16) for b in range(i + 1)
            ]
            dq_t = sum(dot(kt[unit, :, key], dscore[b]) for b, key in enumerate(keys))
            grads[unit, rows, cols] = (dq_t * scaling).T.astype(BF16)
            all_probs.append(probs)
            all_dscore.append(dscore)
        both_q = jnp.concatenate(plain, axis=0)
        both_grad = jnp.concatenate(gradients, axis=0)
        for b, key in enumerate(keys):
            more_k = dot(jnp.concatenate([part_[b] for part_ in all_dscore], axis=1), both_q)
            more_v = dot(jnp.concatenate([part_[b] for part_ in all_probs], axis=1), both_grad)
            dk[unit, key, :] = more_k if b == i else dk[unit, key, :] + more_k
            dv[unit, key, :] = more_v if b == i else dv[unit, key, :] + more_v
        at = pl.ds(i * BLOCK, BLOCK)
        stores.start(att.at[unit, at], att_refs[unit].at[at])
        if i == steps - 1:
            grads[unit, :, 256:384] = (dk[unit] * scaling).astype(BF16)
            grads[unit, :, 384:512] = dv[unit].astype(BF16)
            for s in range(seq):
                to = part(lax.rem(me + s, seq), tok)
                stores.start(grads.at[unit, to], gs[s].at[rows_at[unit]])
    stores.wait()


def rows_call(where, xs, grad_whole, grad_row, marks, seq):
    tok = xs[0].shape[1]
    length = seq * tok
    f32 = jnp.float32
    out = call(
        functools.partial(rows_kernel, seq, tok),
        (where, *[xs[s] for s in (0, *ORDER_IN)], grad_whole, grad_row, *marks),
        [
            jax.ShapeDtypeStruct((2, length, 256), BF16),
            jax.ShapeDtypeStruct((length, 256), BF16),
        ]
        + [jax.ShapeDtypeStruct((2, tok, 512), BF16)] * seq,
        [
            pltpu.VMEM((2, length, 512), BF16),
            pltpu.VMEM((2, length, 256), BF16),
            pltpu.VMEM((2, length, HD), BF16),
            pltpu.VMEM((2, length, 256), BF16),
            pltpu.VMEM((2, HD, length), BF16),
            pltpu.VMEM((2, HD, length), BF16),
            pltpu.VMEM((2, length, HD), f32),
            pltpu.VMEM((2, length, HD), f32),
            pltpu.VMEM((2, length, 256), BF16),
            pltpu.VMEM((2, length, 512), BF16),
            pltpu.SemaphoreType.DMA((2, seq + 3)),
            pltpu.SemaphoreType.DMA((2 * (seq + length // BLOCK),)),
        ],
        "rows",
        flops=2 * 10**10,
        nbytes=MIB,
    )
    return out[0], out[1], out[2:]


def unpack_kernel(seq, where, *refs):
    parts = dict(zip((0, *ORDER_OUT), refs))
    row_ref, refs = refs[seq], refs[seq + 2 :]
    att, gq, gk, gv, near, wide, sums, held, sems_in, sems_out = refs
    me, *rows = places(where)
    loads, stores = Copies(sems_in), Copies(sems_out)
    for s in range(seq):
        origin = lax.rem(me + seq - s, seq)
        loads.start(parts[s].at[:, :, pl.ds(256, 256)], near.at[origin])
    for s in range(seq):
        origin = lax.rem(me + seq - s, seq)
        loads.start(parts[s].at[:, :, pl.ds(0, 256)], wide.at[:, :, part(origin, 256)])
    loads.start(row_ref, held)
    loads.wait(0, seq)
    for head in range(KVH):
        both = near[2 * head].astype(jnp.float32) + near[2 * head + 1].astype(jnp.float32)
        both = both.astype(BF16)
        cols = slice(head * HD, (head + 1) * HD)
        sums[0, :, :, cols] = both[:, :, 0:HD]
        sums[1, :, :, cols] = both[:, :, HD:]
    stores.start(sums.at[0], gk)
    stores.start(sums.at[1], gv)
    loads.wait(seq)
    stores.start(wide, gq)
    stores.start(held, att.at[rows[1]])
    stores.wait()


def unpack(where, parts, row, attended, seq):
    tok = parts[0].shape[1]
    return call(
        functools.partial(unpack_kernel, seq),
        (where, *[parts[s] for s in (0, *ORDER_OUT)], row, attended),
        [
            jax.ShapeDtypeStruct(attended.shape, BF16),
            jax.ShapeDtypeStruct((2, tok, QH * HD), BF16),
            jax.ShapeDtypeStruct((2, tok, KVH * HD), BF16),
            jax.ShapeDtypeStruct((2, tok, KVH * HD), BF16),
        ],
        [
            pltpu.VMEM((seq, 2, tok, 256), BF16),
            pltpu.VMEM((2, tok, QH * HD), BF16),
            pltpu.VMEM((2, 2, tok, KVH * HD), BF16),
            pltpu.VMEM(row.shape, BF16),
            pltpu.SemaphoreType.DMA((2 * seq + 1,)),
            pltpu.SemaphoreType.DMA((4,)),
        ],
        "unpack",
        limit=16,
        aliases={2 + seq: 0},
    )


def route_kernel(groups, partner, spread, *refs):
    routed, held, sems = refs[-3:]
    copies = Copies(sems)
    for group in range(groups):
        copies.start(spread.at[partner[group]], held.at[group])
    copies.wait()
    copies.start(held, routed).wait()


def route(partner, spread, after=()):
    groups = spread.shape[0]
    return call(
        functools.partial(route_kernel, groups),
        (partner, spread, *after),
        [jax.ShapeDtypeStruct(spread.shape, spread.dtype)],
        [pltpu.VMEM(spread.shape, spread.dtype), pltpu.SemaphoreType.DMA((groups + 1,))],
        "route",
        limit=8,
    )[0]


def shifted(arrays, seq, order):
    out = {0: arrays[0]}
    for s in order:
        out[s] = lax.ppermute(arrays[s], "seq", [(d, (d + s) % seq) for d in range(seq)])
    return [out[s] for s in range(seq)], tuple(out[s] for s in order)


def swapped(row, partner, after=()):
    groups = lax.axis_size("dp")
    shape = row.shape
    pieces = row.reshape(groups, shape[0] // groups, shape[1])
    spread = lax.all_to_all(pieces, "dp", 0, 0, tiled=True)
    routed = route(partner, spread, after)
    return lax.all_to_all(routed, "dp", 0, 0, tiled=True).reshape(shape)


def per_device(queries, key_states, value_states, grad_out, doc_ids, partner, swap_rows):
    seq = lax.axis_size("seq")
    group = lax.axis_index("dp")
    moving = swap_rows[group, 0]
    staying = 1 - moving
    where = swap_rows.reshape(1, -1)
    docs = lax.dynamic_slice_in_dim(doc_ids, group * 2, 2, 0)
    lanes = jnp.arange(HD, dtype=jnp.int32)

    def marks(row):
        same = lax.dynamic_index_in_dim(docs, row, 0, False)[:, None] == lanes
        return jnp.where(same, 0.0, FAR).astype(BF16), same.astype(BF16)

    sent, grad_row = pack(where, queries, key_states, value_states, grad_out, seq)
    got, _ = shifted(sent, seq, ORDER_IN)
    grad_move = swapped(grad_row, partner)
    attended, att_move, back = rows_call(
        where, got, grad_out, grad_move, (*marks(staying), *marks(moving)), seq
    )
    returned, early = shifted(back, seq, ORDER_OUT)
    att_move = swapped(att_move, partner)
    return unpack(where, returned, att_move, attended, seq)


def solution(mesh):
    return jax.shard_map(
        per_device,
        mesh=mesh,
        in_specs=(
            P("dp", "seq", None),
            P("dp", "seq", None),
            P("dp", "seq", None),
            P("dp", None, "seq"),
            P(),
            P(),
            P(),
        ),
        out_specs=(
            P("dp", None, "seq"),
            P("dp", "seq", None),
            P("dp", "seq", None),
            P("dp", "seq", None),
        ),
        check_vma=False,
    )
```

```python
import functools

import jax
import jax.numpy as jnp
from jax import lax
from jax.experimental import pallas as pl
from jax.experimental.pallas import tpu as pltpu
from jax.sharding import PartitionSpec as P

QH = 16
KVH = 4
HD = 128
BLOCK = 256
FAR = -1e30
ORDER_IN = (1, 7, 4, 3, 5, 2, 6)
ORDER_OUT = (3, 5, 2, 6, 4, 1, 7)
ANY = pl.BlockSpec(memory_space=pl.ANY)
HBM = pl.BlockSpec(memory_space=pltpu.HBM)
SMEM = pl.BlockSpec(memory_space=pltpu.SMEM)
MIB = 1024 * 1024
BF16 = jnp.bfloat16


def dot(a, b, dims=((1,), (0,))):
    return lax.dot_general(a, b, (dims, ((), ())), preferred_element_type=jnp.float32)


def part(index, size):
    return pl.ds(pl.multiple_of(index * size, size), size)


def places(swap_rows):
    moving = swap_rows[0, lax.axis_index("dp")]
    return lax.axis_index("seq"), 1 - moving, moving


class Copies:
    def __init__(self, sems):
        self.sems, self.all = sems, []

    def start(self, source, target):
        copy = pltpu.make_async_copy(source, target, self.sems.at[len(self.all)])
        copy.start()
        self.all.append(copy)
        return copy

    def wait(self, begin=0, end=None):
        for copy in self.all[begin:end]:
            copy.wait()


def call(kernel, operands, outs, scratch, name, aliases=None, limit=60, flops=0, nbytes=2 * MIB):
    return pl.pallas_call(
        kernel,
        out_shape=outs,
        in_specs=[SMEM] + [HBM] * (len(operands) - 1),
        out_specs=[HBM] * len(outs),
        scratch_shapes=scratch,
        input_output_aliases=aliases or {},
        compiler_params=pltpu.CompilerParams(vmem_limit_bytes=limit * MIB),
        cost_estimate=pl.CostEstimate(flops=flops, bytes_accessed=nbytes, transcendentals=0),
        name=name,
    )(*operands)


def pack_kernel(seq, where, q_ref, k_ref, v_ref, grad_ref, *refs):
    outs, grad_out, (chunks, grad, sems_in, sems_out) = refs[:seq], refs[seq], refs[-4:]
    me, *rows = places(where)
    loads, stores = Copies(sems_in), Copies(sems_out)
    order = (*ORDER_IN, 0)
    for s in order:
        to = lax.rem(me + s, seq)
        head, chunk = part(to // 2, HD), chunks.at[s]
        loads.start(q_ref.at[:, :, part(to, 256)], chunk.at[:, :, pl.ds(0, 256)])
        loads.start(k_ref.at[:, :, head], chunk.at[:, :, pl.ds(256, HD)])
        loads.start(v_ref.at[:, :, head], chunk.at[:, :, pl.ds(384, HD)])
        if s == order[0]:
            loads.start(grad_ref.at[rows[1]], grad)
    at = 0
    for s in order:
        loads.wait(at, at + 3)
        stores.start(chunks.at[s], outs[s])
        at += 3
        if s == order[0]:
            loads.wait(at, at + 1)
            stores.start(grad, grad_out)
            at += 1
    stores.wait()


def pack(where, q, k, v, grad, seq):
    tok, length = q.shape[1], grad.shape[1]
    out = call(
        functools.partial(pack_kernel, seq),
        (where, q, k, v, grad),
        [jax.ShapeDtypeStruct((2, tok, 512), BF16)] * seq
        + [jax.ShapeDtypeStruct((length, 256), BF16)],
        [
            pltpu.VMEM((seq, 2, tok, 512), BF16),
            pltpu.VMEM((length, 256), BF16),
            pltpu.SemaphoreType.DMA((3 * seq + 1,)),
            pltpu.SemaphoreType.DMA((seq + 1,)),
        ],
        "pack",
    )
    return out[:seq], out[seq]


def rows_kernel(seq, tok, where, *refs):
    xs, refs = dict(zip((0, *ORDER_IN), refs)), refs[seq:]
    grad_whole, grad_row, marks, att_whole, att_row = refs[0], refs[1], refs[2:6], refs[6], refs[7]
    gs, refs = refs[8 : 8 + seq], refs[8 + seq :]
    x_s, ka, qm, do, kt, vt, dk, dv, att, grads, sems_in, sems_out = refs
    me, *rows_at = places(where)
    length = seq * tok
    steps = length // BLOCK
    per = BLOCK // tok
    scaling = float(HD) ** (-0.5)
    to_log2 = scaling * 1.4426950408889634
    grad_refs = grad_whole.at[rows_at[0]], grad_row
    att_refs = att_whole.at[rows_at[0]], att_row

    def chunk_copy(unit, s, origin):
        return pltpu.make_async_copy(
            xs[s].at[rows_at[unit]], x_s.at[unit, part(origin, tok)], sems_in.at[unit, origin]
        )

    def whole_copies(unit):
        every = [
            (marks[2 * unit], qm.at[unit]),
            (marks[2 * unit + 1], ka.at[unit, :, pl.ds(HD, HD)]),
            (grad_refs[unit], do.at[unit]),
        ]
        return [
            pltpu.make_async_copy(source, target, sems_in.at[unit, seq + n])
            for n, (source, target) in enumerate(every)
        ]

    for unit in range(2):
        for copy in whole_copies(unit):
            copy.start()
        for s in range(seq):
            chunk_copy(unit, s, lax.rem(me + seq - s, seq)).start()
    key_at = lax.broadcasted_iota(jnp.int32, (BLOCK, BLOCK), 0)
    query_at = lax.broadcasted_iota(jnp.int32, (BLOCK, BLOCK), 1)
    causal = key_at <= query_at
    stores = Copies(sems_out)
    for unit, i in [(unit, i) for unit in range(2) for i in range(steps)]:
        rows = slice(i * BLOCK, (i + 1) * BLOCK)
        keys = [slice(b * BLOCK, (b + 1) * BLOCK) for b in range(i + 1)]
        if i == 0:
            for copy in whole_copies(unit):
                copy.wait()
        for origin in range(i * per, (i + 1) * per):
            chunk_copy(unit, 0, origin).wait()
        ka[unit, rows, 0:HD] = x_s[unit, rows, 256:384]
        kt[unit, :, rows] = x_s[unit, rows, 256:384].T
        vt[unit, :, rows] = x_s[unit, rows, 384:512].T
        mark = qm[unit, rows, :]
        plain = [x_s[unit, rows, h * HD : (h + 1) * HD] for h in range(2)]
        queries = [jnp.concatenate([query, mark], axis=1) for query in plain]
        gradients = [do[unit, rows, h * HD : (h + 1) * HD] for h in range(2)]
        scores, grad_probs = [], []
        for h in range(2):
            blocks = [dot(ka[unit, key, :], queries[h], ((1,), (1,))) for key in keys]
            blocks[i] = jnp.where(causal, blocks[i], FAR)
            scores.append(blocks)
        for h in range(2):
            grad_t = gradients[h].T
            grad_probs.append([dot(x_s[unit, key, 384:512], grad_t) for key in keys])
        all_probs, all_dscore = [], []
        for h in range(2):
            cols = slice(h * HD, (h + 1) * HD)
            top = functools.reduce(
                jnp.maximum, [jnp.max(block, axis=0, keepdims=True) for block in scores[h]]
            )
            expo = [jnp.exp2((block - top) * to_log2) for block in scores[h]]
            total = sum(jnp.sum(block, axis=0, keepdims=True) for block in expo)
            inverse = 1.0 / total
            weights = [block * inverse for block in expo]
            probs = [block.astype(BF16) for block in weights]
            out_t = sum(dot(vt[unit, :, key], probs[b]) for b, key in enumerate(keys))
            att[unit, rows, cols] = out_t.T.astype(BF16)
            grad_t = gradients[h].T.astype(jnp.float32)
            inner = jnp.sum(grad_t * out_t, axis=0, keepdims=True)
            dscore = [
                (weights[b] * (grad_probs[h][b] - inner)).astype(BF16) for b in range(i + 1)
            ]
            dq_t = sum(dot(kt[unit, :, key], dscore[b]) for b, key in enumerate(keys))
            grads[unit, rows, cols] = (dq_t * scaling).T.astype(BF16)
            all_probs.append(probs)
            all_dscore.append(dscore)
        both_q = jnp.concatenate(plain, axis=0)
        both_grad = jnp.concatenate(gradients, axis=0)
        for b, key in enumerate(keys):
            more_k = dot(jnp.concatenate([part_[b] for part_ in all_dscore], axis=1), both_q)
            more_v = dot(jnp.concatenate([part_[b] for part_ in all_probs], axis=1), both_grad)
            dk[unit, key, :] = more_k if b == i else dk[unit, key, :] + more_k
            dv[unit, key, :] = more_v if b == i else dv[unit, key, :] + more_v
        at = pl.ds(i * BLOCK, BLOCK)
        stores.start(att.at[unit, at], att_refs[unit].at[at])
        if i == steps - 1:
            grads[unit, :, 256:384] = (dk[unit] * scaling).astype(BF16)
            grads[unit, :, 384:512] = dv[unit].astype(BF16)
            for s in range(seq):
                to = part(lax.rem(me + s, seq), tok)
                stores.start(grads.at[unit, to], gs[s].at[rows_at[unit]])
    stores.wait()


def rows_call(where, xs, grad_whole, grad_row, marks, seq):
    tok = xs[0].shape[1]
    length = seq * tok
    f32 = jnp.float32
    out = call(
        functools.partial(rows_kernel, seq, tok),
        (where, *[xs[s] for s in (0, *ORDER_IN)], grad_whole, grad_row, *marks),
        [
            jax.ShapeDtypeStruct((2, length, 256), BF16),
            jax.ShapeDtypeStruct((length, 256), BF16),
        ]
        + [jax.ShapeDtypeStruct((2, tok, 512), BF16)] * seq,
        [
            pltpu.VMEM((2, length, 512), BF16),
            pltpu.VMEM((2, length, 256), BF16),
            pltpu.VMEM((2, length, HD), BF16),
            pltpu.VMEM((2, length, 256), BF16),
            pltpu.VMEM((2, HD, length), BF16),
            pltpu.VMEM((2, HD, length), BF16),
            pltpu.VMEM((2, length, HD), f32),
            pltpu.VMEM((2, length, HD), f32),
            pltpu.VMEM((2, length, 256), BF16),
            pltpu.VMEM((2, length, 512), BF16),
            pltpu.SemaphoreType.DMA((2, seq + 3)),
            pltpu.SemaphoreType.DMA((2 * (seq + length // BLOCK),)),
        ],
        "rows",
        flops=2 * 10**10,
        nbytes=MIB,
    )
    return out[0], out[1], out[2:]


def unpack_kernel(seq, where, *refs):
    parts = dict(zip((0, *ORDER_OUT), refs))
    row_ref, refs = refs[seq], refs[seq + 2 :]
    att, gq, gk, gv, near, wide, sums, held, sems_in, sems_out = refs
    me, *rows = places(where)
    loads, stores = Copies(sems_in), Copies(sems_out)
    for s in range(seq):
        origin = lax.rem(me + seq - s, seq)
        loads.start(parts[s].at[:, :, pl.ds(256, 256)], near.at[origin])
    for s in range(seq):
        origin = lax.rem(me + seq - s, seq)
        loads.start(parts[s].at[:, :, pl.ds(0, 256)], wide.at[:, :, part(origin, 256)])
    loads.start(row_ref, held)
    loads.wait(0, seq)
    for head in range(KVH):
        both = near[2 * head].astype(jnp.float32) + near[2 * head + 1].astype(jnp.float32)
        both = both.astype(BF16)
        cols = slice(head * HD, (head + 1) * HD)
        sums[0, :, :, cols] = both[:, :, 0:HD]
        sums[1, :, :, cols] = both[:, :, HD:]
    stores.start(sums.at[0], gk)
    stores.start(sums.at[1], gv)
    for s in range(seq):
        loads.wait(seq + s, seq + s + 1)
        cols = part(lax.rem(me + seq - s, seq), 256)
        stores.start(wide.at[:, :, cols], gq.at[:, :, cols])
    loads.wait(2 * seq)
    stores.start(held, att.at[rows[1]])
    stores.wait()


def unpack(where, parts, row, attended, seq):
    tok = parts[0].shape[1]
    return call(
        functools.partial(unpack_kernel, seq),
        (where, *[parts[s] for s in (0, *ORDER_OUT)], row, attended),
        [
            jax.ShapeDtypeStruct(attended.shape, BF16),
            jax.ShapeDtypeStruct((2, tok, QH * HD), BF16),
            jax.ShapeDtypeStruct((2, tok, KVH * HD), BF16),
            jax.ShapeDtypeStruct((2, tok, KVH * HD), BF16),
        ],
        [
            pltpu.VMEM((seq, 2, tok, 256), BF16),
            pltpu.VMEM((2, tok, QH * HD), BF16),
            pltpu.VMEM((2, 2, tok, KVH * HD), BF16),
            pltpu.VMEM(row.shape, BF16),
            pltpu.SemaphoreType.DMA((2 * seq + 1,)),
            pltpu.SemaphoreType.DMA((seq + 3,)),
        ],
        "unpack",
        limit=16,
        aliases={2 + seq: 0},
    )


def route_kernel(groups, partner, spread, *refs):
    routed, held, sems = refs[-3:]
    copies = Copies(sems)
    for group in range(groups):
        copies.start(spread.at[partner[group]], held.at[group])
    copies.wait()
    copies.start(held, routed).wait()


def route(partner, spread, after=()):
    groups = spread.shape[0]
    return call(
        functools.partial(route_kernel, groups),
        (partner, spread, *after),
        [jax.ShapeDtypeStruct(spread.shape, spread.dtype)],
        [pltpu.VMEM(spread.shape, spread.dtype), pltpu.SemaphoreType.DMA((groups + 1,))],
        "route",
        limit=8,
    )[0]


def shifted(arrays, seq, order):
    out = {0: arrays[0]}
    for s in order:
        out[s] = lax.ppermute(arrays[s], "seq", [(d, (d + s) % seq) for d in range(seq)])
    return [out[s] for s in range(seq)], tuple(out[s] for s in order)


def swapped(row, partner, after=()):
    groups = lax.axis_size("dp")
    shape = row.shape
    pieces = row.reshape(groups, shape[0] // groups, shape[1])
    spread = lax.all_to_all(pieces, "dp", 0, 0, tiled=True)
    routed = route(partner, spread, after)
    return lax.all_to_all(routed, "dp", 0, 0, tiled=True).reshape(shape)


def per_device(queries, key_states, value_states, grad_out, doc_ids, partner, swap_rows):
    seq = lax.axis_size("seq")
    group = lax.axis_index("dp")
    moving = swap_rows[group, 0]
    staying = 1 - moving
    where = swap_rows.reshape(1, -1)
    docs = lax.dynamic_slice_in_dim(doc_ids, group * 2, 2, 0)
    lanes = jnp.arange(HD, dtype=jnp.int32)

    def marks(row):
        same = lax.dynamic_index_in_dim(docs, row, 0, False)[:, None] == lanes
        return jnp.where(same, 0.0, FAR).astype(BF16), same.astype(BF16)

    sent, grad_row = pack(where, queries, key_states, value_states, grad_out, seq)
    got, _ = shifted(sent, seq, ORDER_IN)
    grad_move = swapped(grad_row, partner)
    attended, att_move, back = rows_call(
        where, got, grad_out, grad_move, (*marks(staying), *marks(moving)), seq
    )
    returned, early = shifted(back, seq, ORDER_OUT)
    att_move = swapped(att_move, partner)
    return unpack(where, returned, att_move, attended, seq)


def solution(mesh):
    return jax.shard_map(
        per_device,
        mesh=mesh,
        in_specs=(
            P("dp", "seq", None),
            P("dp", "seq", None),
            P("dp", "seq", None),
            P("dp", None, "seq"),
            P(),
            P(),
            P(),
        ),
        out_specs=(
            P("dp", None, "seq"),
            P("dp", "seq", None),
            P("dp", "seq", None),
            P("dp", "seq", None),
        ),
        check_vma=False,
    )
```
